32 devices in a mesh: row: 8 (over z, x), col: 4 (over y, core).
Axes of the slice: x: 2, y: 2, z: 4, core: 2. Of those that a mesh axis runs over, the one named last changes fastest.
Arguments:
- measured: bfloat16 [128, 32, 16, 512], P('col', 'row'), may hold values from 0 to 2
- module_row: int32 [32], replicated, may hold values from 0 to 31, each once
- scan_offsets: int32 [8, 4, 4, 2], P('row', 'col'), may hold values from 0 to 511, as said below
- specimen: float32 [2, 2048, 2048], P(None, 'row', 'col'), may hold values from -9.3 to 9.3
- illumination: float32 [2, 512, 512], replicated, may hold values from -4 to 4
Outputs:
- specimen_step: float32 [2, 2048, 2048], P(None, 'row', 'col')
- illumination_step: float32 [2, 512, 512], replicated
The draws below stay inside these ranges and needn't reach their ends.
Inputs may be any that keep to these rules, and one draw needn't show every extreme that they name: `scan_offsets`: position s of a device's tile has row offset in [0, 256) and column offset in [s * 128, (s + 1) * 128).
All inputs are finite; a program needn't handle non-finite values.
Results may differ from the reference program's by a relative error of at most 0.002.
The reference program's roundings to bfloat16 on the way count: a program that leaves them out, or rounds other values in their place, can miss the bound.
Values may be sent and summed in bfloat16 or wider, within the bound.
A program may use at most 128 MiB of HBM per device.

```python
import math
import jax
import jax.numpy as jnp
from jax import lax

FRAME = 512
MODULES = 32
SLOTS = 4
TY = 256
TX = 512
MROWS = 16
NOY = 2048
NOX = 2048
POSITIONS = 128
N_ROW = 8
N_COL = 4


def draw_scan_offsets(key, part):
    first, second = jax.random.split(key)
    rows_part = jax.random.randint(first, (N_ROW, N_COL, SLOTS), 0, TY, dtype=jnp.int32)
    width = TX // SLOTS
    cols_part = jax.random.randint(second, (N_ROW, N_COL, SLOTS), 0, width, dtype=jnp.int32)
    rows_part = rows_part.at[0, 0, 0].set(TY - 1)
    cols_part = cols_part.at[0, 0, 0].set(0)
    cols_part = cols_part.at[N_ROW - 1, N_COL - 1, SLOTS - 1].set(width - 1)
    cols_part = cols_part + jnp.arange(SLOTS, dtype=jnp.int32)[None, None, :] * width
    return jnp.stack([rows_part, cols_part], axis=-1)


def draw_specimen(key, part):
    first, second = jax.random.split(key)
    scale = jnp.exp(jax.random.uniform(first, (NOY, NOX), jnp.float32, -1.2, 1.2))
    values = 0.7 * jnp.clip(jax.random.normal(second, (2, NOY, NOX), jnp.float32), -4.0, 4.0)
    return values * scale[None]


def level_of(own_key, dims, cuts, least, top_value):
    def one(axis_at, blocks):
        steps = jax.random.uniform(jax.random.fold_in(jax.random.fold_in(own_key, 6), axis_at), (blocks,), jnp.float32, least / len(cuts), top_value / len(cuts))
        return jnp.repeat(jnp.exp(steps), dims[axis_at] // blocks).reshape((-1,) + (1,) * (len(dims) - axis_at - 1))

    level = one(*cuts[0])
    for cut in cuts[1:]:
        level = level * one(*cut)
    return level


def normal_values(stream_key, shape, spread, most, kind=jnp.bfloat16):
    drawn = jax.random.normal(stream_key, shape, jnp.float32) * spread
    return jnp.minimum(jnp.maximum(drawn, -most), most).astype(kind)


def setup_inputs(seed: int = 0) -> dict:
    key_list = jax.random.split(jax.random.key(seed), 6)
    measured = jnp.clip(2.0 * jax.random.uniform(key_list[0], (POSITIONS, MODULES, MROWS, FRAME), jnp.float32) ** level_of(key_list[0], (POSITIONS, MODULES, MROWS, FRAME), ((0, 4), (1, 8)), -0.2, 0.2), 0.0, 2.0).astype(jnp.bfloat16)
    module_row = jax.random.permutation(key_list[1], MODULES).astype(jnp.int32)
    scan_offsets = draw_scan_offsets(jax.random.fold_in(key_list[5], 71), 0)
    specimen = draw_specimen(jax.random.fold_in(key_list[5], 71), 0)
    illumination = normal_values(key_list[4], (2, FRAME, FRAME), 0.7, 4.0, jnp.float32)
    return {"measured": measured, "module_row": module_row, "scan_offsets": scan_offsets, "specimen": specimen, "illumination": illumination}


def dft_tables(size):
    index = jnp.arange(size, dtype=jnp.int32)
    wrapped = index[:, None] * index[None, :] % size
    angle = wrapped.astype(jnp.float32) * (2.0 * math.pi / size)
    norm = 1.0 / math.sqrt(size)
    return ((jnp.cos(angle) * norm).astype(jnp.bfloat16), (-jnp.sin(angle) * norm).astype(jnp.bfloat16))

def mdot(left, right):
    return jnp.dot(left, right, preferred_element_type=jnp.float32)

def reference(measured, module_row, scan_offsets, specimen, illumination):
    inverse = jnp.zeros((MODULES,), jnp.int32).at[module_row].set(jnp.arange(MODULES, dtype=jnp.int32))
    amplitude = jnp.take(measured, inverse, axis=1).reshape(POSITIONS, FRAME, FRAME)
    rows_index = jnp.arange(N_ROW, dtype=jnp.int32)
    cols_index = jnp.arange(N_COL, dtype=jnp.int32)
    offsets = jnp.transpose(scan_offsets, (1, 0, 2, 3))
    anchor_rows = (rows_index[None, :, None] * TY + offsets[..., 0]).reshape(POSITIONS).astype(jnp.int32)
    anchor_cols = (cols_index[:, None, None] * TX + offsets[..., 1]).reshape(POSITIONS).astype(jnp.int32)
    wide = jnp.concatenate([specimen, specimen[:, :, :FRAME]], axis=2)
    wide = jnp.concatenate([wide, wide[:, :FRAME]], axis=1)
    cos_table, sin_table = dft_tables(FRAME)
    ill_real = illumination[0]
    ill_imag = illumination[1]
    zero = jnp.zeros((), jnp.int32)

    def one_position(carry, inputs):
        accum, num_real, num_imag, density = carry
        amp, row_at, col_at = inputs
        patch = lax.dynamic_slice(wide, (zero, row_at, col_at), (2, FRAME, FRAME))
        spec_real = patch[0]
        spec_imag = patch[1]
        wave_real = (ill_real * spec_real - ill_imag * spec_imag).astype(jnp.bfloat16)
        wave_imag = (ill_real * spec_imag + ill_imag * spec_real).astype(jnp.bfloat16)
        half_real = (mdot(cos_table, wave_real) - mdot(sin_table, wave_imag)).astype(jnp.bfloat16)
        half_imag = (mdot(cos_table, wave_imag) + mdot(sin_table, wave_real)).astype(jnp.bfloat16)
        far_real = mdot(half_real, cos_table) - mdot(half_imag, sin_table)
        far_imag = mdot(half_real, sin_table) + mdot(half_imag, cos_table)
        magnitude = jnp.sqrt(far_real * far_real + far_imag * far_imag)
        factor = amp.astype(jnp.float32) / jnp.maximum(magnitude, 0.25) - 1.0
        corr_real = (factor * far_real).astype(jnp.bfloat16)
        corr_imag = (factor * far_imag).astype(jnp.bfloat16)
        back_real = (mdot(cos_table, corr_real) + mdot(sin_table, corr_imag)).astype(jnp.bfloat16)
        back_imag = (mdot(cos_table, corr_imag) - mdot(sin_table, corr_real)).astype(jnp.bfloat16)
        chg_real = mdot(back_real, cos_table) + mdot(back_imag, sin_table)
        chg_imag = mdot(back_imag, cos_table) - mdot(back_real, sin_table)
        grad = jnp.stack([ill_real * chg_real + ill_imag * chg_imag, ill_real * chg_imag - ill_imag * chg_real])
        current = lax.dynamic_slice(accum, (zero, row_at, col_at), (2, FRAME, FRAME))
        accum = lax.dynamic_update_slice(accum, current + grad, (zero, row_at, col_at))
        num_real = num_real + spec_real * chg_real + spec_imag * chg_imag
        num_imag = num_imag + spec_real * chg_imag - spec_imag * chg_real
        density = density + spec_real * spec_real + spec_imag * spec_imag
        return ((accum, num_real, num_imag, density), None)
    start = (jnp.zeros((2, NOY + FRAME, NOX + FRAME), jnp.float32), jnp.zeros((FRAME, FRAME), jnp.float32), jnp.zeros((FRAME, FRAME), jnp.float32), jnp.zeros((FRAME, FRAME), jnp.float32))
    (accum, num_real, num_imag, density), _ = lax.scan(one_position, start, (amplitude, anchor_rows, anchor_cols))
    specimen_step = accum[:, :NOY, :NOX]
    specimen_step = specimen_step.at[:, :FRAME, :].add(accum[:, NOY:, :NOX])
    specimen_step = specimen_step.at[:, :, :FRAME].add(accum[:, :NOY, NOX:])
    specimen_step = specimen_step.at[:, :FRAME, :FRAME].add(accum[:, NOY:, NOX:])
    root = jnp.sqrt(density + 1e-06)
    illumination_step = jnp.stack([num_real / root, num_imag / root])
    return (specimen_step, illumination_step)
```

```python
import functools
import math

import jax
import jax.numpy as jnp
from jax import lax
from jax.experimental import pallas as pl
from jax.experimental.pallas import tpu as pltpu
from jax.sharding import PartitionSpec as P

VMEM_LIMIT = 56 * 2**20
LANES = 128
SUBLANES = 8


def passed_along(value, axis, steps):
    count = lax.axis_size(axis)
    pairs = [(source, (source + steps) % count) for source in range(count)]
    return lax.ppermute(value, axis, pairs)


def dft_tables(size):
    index = jnp.arange(size, dtype=jnp.int32)
    wrapped = index[:, None] * index[None, :] % size
    angle = wrapped.astype(jnp.float32) * (2.0 * math.pi / size)
    norm = 1.0 / math.sqrt(size)
    return (
        (jnp.cos(angle) * norm).astype(jnp.bfloat16),
        (-jnp.sin(angle) * norm).astype(jnp.bfloat16),
    )


def mdot(left, right):
    return jnp.dot(left, right, preferred_element_type=jnp.float32)


def forward_kernel(
    offsets, t00, t01, t10, t11, t20, t21, ill, left, right, far, patch, density, region, wave, half, sems
):
    slot = pl.program_id(0)
    size = ill.shape[-1]
    rows, cols = t00.shape[1:]
    wide = size + LANES
    step = 64

    @pl.when(slot == 0)
    def _():
        copies = []
        for at, tile in enumerate((t00, t01, t10, t11, t20, t21)):
            down, across = divmod(at, 2)
            place = region.at[:, pl.ds(down * rows, rows), pl.ds(across * cols, cols)]
            copies.append(pltpu.make_async_copy(tile, place, sems.at[at]))
        for copy in copies:
            copy.start()
        for copy in copies:
            copy.wait()
        density[...] = jnp.zeros_like(density)

    row_at = offsets[slot, 0]
    fine = lax.rem(row_at, SUBLANES)
    coarse = row_at - fine
    tall = step + SUBLANES
    base = pl.multiple_of(slot * (cols // pl.num_programs(0)), LANES)
    shift = lax.rem(wide - (offsets[slot, 1] - base), wide)
    raised = lax.rem(tall - fine, tall)

    def gather(i, carry):
        at = pl.multiple_of(i * step, step)
        here = pl.ds(at, step)
        parts = []
        for part in range(2):
            top = pl.multiple_of(coarse + at, SUBLANES)
            block = region[part, pl.ds(top, tall), pl.ds(base, wide)]
            moved = pltpu.roll(block, shift, 1)[:, :size]
            parts.append(pltpu.roll(moved, raised, 0)[:step])
        real, imag = parts
        patch[0, 0, here, :] = real
        patch[0, 1, here, :] = imag
        density[here, :] += real * real + imag * imag
        ill_real = ill[0, here, :]
        ill_imag = ill[1, here, :]
        wave[here, :] = (ill_real * real - ill_imag * imag).astype(jnp.bfloat16)
        low = pl.ds(pl.multiple_of(size + at, step), step)
        wave[low, :] = (ill_real * imag + ill_imag * real).astype(jnp.bfloat16)
        return carry

    lax.fori_loop(0, size // step, gather, 0)
    half[:, :size] = mdot(left[:size, :], wave[...]).astype(jnp.bfloat16)
    half[:, size:] = mdot(left[size:, :], wave[...]).astype(jnp.bfloat16)
    far[0] = mdot(half[...], right[...])


def backward_kernel(
    offsets, module_row, amp, far, patch, ill, left, right, upper, middle, lower, side, numer,
    frame, accum, corr, back, change,
):
    slot = pl.program_id(0)
    size = ill.shape[-1]
    rows, cols = upper.shape[1:]
    wide = size + LANES
    step = 64
    senders, _, own, depth, _ = amp.shape

    @pl.when(slot == 0)
    def _():
        accum[...] = jnp.zeros_like(accum)
        numer[...] = jnp.zeros_like(numer)

    for sender in range(senders):
        for at in range(own):
            top = pl.multiple_of(module_row[sender * own + at] * depth, depth)
            frame[pl.ds(top, depth), :] = amp[sender, 0, at]

    def correct(i, carry):
        at = pl.multiple_of(i * step, step)
        here = pl.ds(at, step)
        real = far[0, here, :size]
        imag = far[0, here, size:]
        magnitude = jnp.sqrt(real * real + imag * imag)
        factor = frame[here, :].astype(jnp.float32) / jnp.maximum(magnitude, 0.25) - 1.0
        corr[here, :] = (factor * real).astype(jnp.bfloat16)
        low = pl.ds(pl.multiple_of(size + at, step), step)
        corr[low, :] = (factor * imag).astype(jnp.bfloat16)
        return carry

    lax.fori_loop(0, size // step, correct, 0)
    back[:, :size] = mdot(right[:size, :], corr[...]).astype(jnp.bfloat16)
    back[:, size:] = mdot(right[size:, :], corr[...]).astype(jnp.bfloat16)
    change[...] = mdot(back[...], left[...])

    row_at = offsets[slot, 0]
    fine = lax.rem(row_at, SUBLANES)
    coarse = row_at - fine
    tall = step + SUBLANES
    base = pl.multiple_of(slot * (cols // pl.num_programs(0)), LANES)
    shift = offsets[slot, 1] - base
    blank_below = jnp.zeros((SUBLANES, size), jnp.float32)
    blank_beside = jnp.zeros((tall, LANES), jnp.float32)

    def spread(i, carry):
        at = pl.multiple_of(i * step, step)
        here = pl.ds(at, step)
        chg_real = change[here, :size]
        chg_imag = change[here, size:]
        ill_real = ill[0, here, :]
        ill_imag = ill[1, here, :]
        real = patch[0, 0, here, :]
        imag = patch[0, 1, here, :]
        numer[0, here, :] += real * chg_real + imag * chg_imag
        numer[1, here, :] += real * chg_imag - imag * chg_real
        grads = (
            ill_real * chg_real + ill_imag * chg_imag,
            ill_real * chg_imag - ill_imag * chg_real,
        )
        for part in range(2):
            moved = pltpu.roll(jnp.concatenate([grads[part], blank_below], axis=0), fine, 0)
            moved = pltpu.roll(jnp.concatenate([moved, blank_beside], axis=1), shift, 1)
            top = pl.multiple_of(coarse + at, SUBLANES)
            accum[part, pl.ds(top, tall), pl.ds(base, wide)] += moved
        return carry

    lax.fori_loop(0, size // step, spread, 0)

    @pl.when(slot == pl.num_programs(0) - 1)
    def _():
        upper[...] = accum[:, :rows, :cols]
        middle[...] = accum[:, rows : 2 * rows, :cols]
        lower[...] = accum[:, 2 * rows :, :cols]
        side[...] = accum[:, :, cols:]


def whole():
    return pl.BlockSpec(memory_space=pltpu.VMEM)


def forward(offsets, tiles, ill, left, right):
    slots = offsets.shape[0]
    size = ill.shape[-1]
    rows, cols = tiles[0].shape[1:]
    return pl.pallas_call(
        forward_kernel,
        grid=(slots,),
        in_specs=[pl.BlockSpec(memory_space=pltpu.SMEM)]
        + [pl.BlockSpec(memory_space=pl.ANY)] * 6
        + [whole()] * 3,
        out_specs=[
            pl.BlockSpec((1, size, 2 * size), lambda s: (s, 0, 0)),
            pl.BlockSpec((1, 2, size, size), lambda s: (s, 0, 0, 0)),
            pl.BlockSpec((size, size), lambda s: (0, 0)),
        ],
        out_shape=[
            jax.ShapeDtypeStruct((slots, size, 2 * size), jnp.float32),
            jax.ShapeDtypeStruct((slots, 2, size, size), jnp.float32),
            jax.ShapeDtypeStruct((size, size), jnp.float32),
        ],
        scratch_shapes=[
            pltpu.VMEM((2, 3 * rows, 2 * cols), jnp.float32),
            pltpu.VMEM((2 * size, size), jnp.bfloat16),
            pltpu.VMEM((size, 2 * size), jnp.bfloat16),
            pltpu.SemaphoreType.DMA((6,)),
        ],
        compiler_params=pltpu.CompilerParams(vmem_limit_bytes=VMEM_LIMIT),
        cost_estimate=pl.CostEstimate(
            flops=16 * slots * size**3, bytes_accessed=28 * 2**20, transcendentals=0
        ),
        name="forward",
    )(offsets, *tiles, ill, left, right)


def backward(offsets, module_row, amp, far, patch, ill, left, right, rows, cols):
    slots = offsets.shape[0]
    size = ill.shape[-1]
    senders, _, own, depth, _ = amp.shape
    scalar = pl.BlockSpec(memory_space=pltpu.SMEM)
    tile = jax.ShapeDtypeStruct((2, rows, cols), jnp.float32)
    return pl.pallas_call(
        backward_kernel,
        grid=(slots,),
        in_specs=[
            scalar,
            scalar,
            pl.BlockSpec((senders, 1, own, depth, size), lambda s: (0, s, 0, 0, 0)),
            pl.BlockSpec((1, size, 2 * size), lambda s: (s, 0, 0)),
            pl.BlockSpec((1, 2, size, size), lambda s: (s, 0, 0, 0)),
            whole(),
            whole(),
            whole(),
        ],
        out_specs=[whole()] * 5,
        out_shape=[
            tile,
            tile,
            tile,
            jax.ShapeDtypeStruct((2, 3 * rows, cols), jnp.float32),
            jax.ShapeDtypeStruct((2, size, size), jnp.float32),
        ],
        scratch_shapes=[
            pltpu.VMEM((size, size), jnp.bfloat16),
            pltpu.VMEM((2, 3 * rows, 2 * cols), jnp.float32),
            pltpu.VMEM((2 * size, size), jnp.bfloat16),
            pltpu.VMEM((size, 2 * size), jnp.bfloat16),
            pltpu.VMEM((size, 2 * size), jnp.float32),
        ],
        compiler_params=pltpu.CompilerParams(vmem_limit_bytes=VMEM_LIMIT),
        cost_estimate=pl.CostEstimate(
            flops=16 * slots * size**3, bytes_accessed=28 * 2**20, transcendentals=0
        ),
        name="backward",
    )(offsets, module_row, amp, far, patch, ill, left, right)


def shard_sum(value, devices):
    parts, size, width = value.shape
    cut = value.reshape(parts, devices, size // devices, width)
    got = lax.all_to_all(cut, ("row", "col"), split_axis=1, concat_axis=1, tiled=True)
    return jnp.sum(got, axis=1)


def shards(measured, module_row, scan_offsets, specimen, illumination):
    slots = scan_offsets.shape[2]
    size = illumination.shape[-1]
    rows, cols = specimen.shape[1:]
    n_row = lax.axis_size("row")
    devices = n_row * lax.axis_size("col")
    offsets = scan_offsets.reshape(slots, 2)
    below = passed_along(specimen, "row", -1)
    farther = passed_along(specimen, "row", -2)
    beside = passed_along(specimen, "col", -1)
    below_beside = passed_along(below, "col", -1)
    farther_beside = passed_along(farther, "col", -1)
    cut = measured.reshape((n_row, slots) + measured.shape[1:])
    amp = lax.all_to_all(cut, "row", split_axis=0, concat_axis=0, tiled=True)
    cos_table, sin_table = dft_tables(size)
    left = jnp.block([[cos_table, -sin_table], [sin_table, cos_table]])
    right = jnp.block([[cos_table, sin_table], [-sin_table, cos_table]])
    tiles = (specimen, beside, below, below_beside, farther, farther_beside)
    far, patch, density = forward(offsets, tiles, illumination, left, right)
    density_share = shard_sum(density[None], devices)
    upper, middle, lower, side, numer = backward(
        offsets, module_row, amp, far, patch, illumination, left, right, rows, cols
    )
    got = passed_along(side, "col", 1)
    middle = middle + got[:, rows : 2 * rows]
    lower = lower + got[:, 2 * rows :]
    specimen_step = (
        upper + got[:, :rows] + passed_along(middle, "row", 1) + passed_along(lower, "row", 2)
    )
    numer_share = shard_sum(numer, devices)
    share = numer_share / jnp.sqrt(density_share + 1e-06)
    illumination_step = lax.all_gather(share, ("row", "col"), axis=1, tiled=True)
    return (specimen_step, illumination_step)


def solution(mesh):
    return jax.shard_map(
        shards,
        mesh=mesh,
        in_specs=(
            P("col", "row", None, None),
            P(),
            P("row", "col", None, None),
            P(None, "row", "col"),
            P(),
        ),
        out_specs=(P(None, "row", "col"), P()),
        check_vma=False,
    )
```

```python
import math

import jax
import jax.numpy as jnp
import ml_dtypes
import numpy as np
from jax import lax
from jax.experimental import pallas as pl
from jax.experimental.pallas import tpu as pltpu
from jax.sharding import PartitionSpec as P

VMEM_LIMIT = 56 * 2**20
LANES = 128
SUBLANES = 8


def passed_along(value, axis, steps):
    count = lax.axis_size(axis)
    pairs = [(source, (source + steps) % count) for source in range(count)]
    return lax.ppermute(value, axis, pairs)


def dft_tables(size):
    index = np.arange(size, dtype=np.int32)
    wrapped = index[:, None] * index[None, :] % size
    angle = wrapped.astype(np.float32) * np.float32(2.0 * math.pi / size)
    norm = np.float32(1.0 / math.sqrt(size))
    return (
        (np.cos(angle) * norm).astype(ml_dtypes.bfloat16),
        (-np.sin(angle) * norm).astype(ml_dtypes.bfloat16),
    )


def pull_lanes(block, off):
    turn = lax.rem(LANES - off, LANES)
    lane = lax.broadcasted_iota(jnp.int32, (block.shape[0], LANES), 1)
    keep = lane < LANES - off
    count = block.shape[1] // LANES
    turned = [pltpu.roll(block[:, i * LANES : (i + 1) * LANES], turn, 1) for i in range(count)]
    return jnp.concatenate(
        [jnp.where(keep, turned[i], turned[i + 1]) for i in range(count - 1)], axis=1
    )


def push_lanes(block, off):
    lane = lax.broadcasted_iota(jnp.int32, (block.shape[0], LANES), 1)
    keep = lane >= off
    count = block.shape[1] // LANES
    blank = jnp.zeros((block.shape[0], LANES), block.dtype)
    turned = [pltpu.roll(block[:, i * LANES : (i + 1) * LANES], off, 1) for i in range(count)]
    turned = [blank] + turned + [blank]
    return jnp.concatenate(
        [jnp.where(keep, turned[i + 1], turned[i]) for i in range(count + 1)], axis=1
    )


def pull_rows(block, off):
    turn = lax.rem(SUBLANES - off, SUBLANES)
    row = lax.broadcasted_iota(jnp.int32, (SUBLANES, block.shape[1]), 0)
    keep = row < SUBLANES - off
    count = block.shape[0] // SUBLANES
    turned = [pltpu.roll(block[i * SUBLANES : (i + 1) * SUBLANES], turn, 0) for i in range(count)]
    return jnp.concatenate(
        [jnp.where(keep, turned[i], turned[i + 1]) for i in range(count - 1)], axis=0
    )


def push_rows(block, off):
    row = lax.broadcasted_iota(jnp.int32, (SUBLANES, block.shape[1]), 0)
    keep = row >= off
    count = block.shape[0] // SUBLANES
    blank = jnp.zeros((SUBLANES, block.shape[1]), block.dtype)
    turned = [pltpu.roll(block[i * SUBLANES : (i + 1) * SUBLANES], off, 0) for i in range(count)]
    turned = [blank] + turned + [blank]
    return jnp.concatenate(
        [jnp.where(keep, turned[i + 1], turned[i]) for i in range(count + 1)], axis=0
    )


def mdot(left, right):
    return jnp.dot(left, right, preferred_element_type=jnp.float32)


def forward_kernel(
    offsets, t00, t01, t10, t10_odd, t11, t20, t21, ill, left, right, far, patch, density_out,
    region, wave, half, density, sems,
):
    slot = pl.program_id(0)
    size = ill.shape[-1]
    rows, cols = t00.shape[1:]
    wide = size + LANES
    step = 64

    @pl.when(slot == 0)
    def _():
        def move(tile, at):
            down, across = divmod(at, 2)
            place = region.at[:, pl.ds(down * rows, rows), pl.ds(across * cols, cols)]
            return pltpu.make_async_copy(tile, place, sems.at[at])

        odd = lax.rem(lax.axis_index("row"), 2) == 1

        @pl.when(odd)
        def _():
            move(t10_odd, 2).start()

        @pl.when(jnp.logical_not(odd))
        def _():
            move(t10, 2).start()

        copies = [move(t00, 0), move(t01, 1), move(t11, 3), move(t20, 4), move(t21, 5)]
        for copy in copies:
            copy.start()
        for copy in copies:
            copy.wait()
        move(t10, 2).wait()
        density[...] = jnp.zeros_like(density)

    row_at = offsets[slot, 0]
    fine = lax.rem(row_at, SUBLANES)
    coarse = row_at - fine
    tall = step + SUBLANES
    base = pl.multiple_of(slot * (cols // pl.num_programs(0)), LANES)
    shift = offsets[slot, 1] - base

    def gather(i, carry):
        at = pl.multiple_of(i * step, step)
        here = pl.ds(at, step)
        parts = []
        for part in range(2):
            top = pl.multiple_of(coarse + at, SUBLANES)
            block = region[part, pl.ds(top, tall), pl.ds(base, wide)]
            parts.append(pull_rows(pull_lanes(block, shift), fine))
        real, imag = parts
        patch[0, 0, here, :] = real
        patch[0, 1, here, :] = imag
        density[here, :] += real * real + imag * imag
        ill_real = ill[0, here, :]
        ill_imag = ill[1, here, :]
        wave[here, :] = (ill_real * real - ill_imag * imag).astype(jnp.bfloat16)
        low = pl.ds(pl.multiple_of(size + at, step), step)
        wave[low, :] = (ill_real * imag + ill_imag * real).astype(jnp.bfloat16)
        return carry

    lax.fori_loop(0, size // step, gather, 0)
    half[:, :size] = mdot(left[:size, :], wave[...]).astype(jnp.bfloat16)
    half[:, size:] = mdot(left[size:, :], wave[...]).astype(jnp.bfloat16)
    far[0] = mdot(half[...], right[...])

    @pl.when(slot == pl.num_programs(0) - 1)
    def _():
        total = density[...].astype(jnp.bfloat16)
        density_out[0] = total
        density_out[1] = total


def backward_kernel(
    offsets, module_row, amp, far, patch, ill, left, right, upper, middle, lower, side, numer_out,
    frame, accum, corr, back, change, numer,
):
    slot = pl.program_id(0)
    size = ill.shape[-1]
    rows, cols = upper.shape[1:]
    wide = size + LANES
    step = 64
    senders, _, own, depth, _ = amp.shape

    @pl.when(slot == 0)
    def _():
        accum[...] = jnp.zeros_like(accum)
        numer[...] = jnp.zeros_like(numer)

    for sender in range(senders):
        for at in range(own):
            top = pl.multiple_of(module_row[sender * own + at] * depth, depth)
            frame[pl.ds(top, depth), :] = amp[sender, 0, at]

    def correct(i, carry):
        at = pl.multiple_of(i * step, step)
        here = pl.ds(at, step)
        real = far[0, here, :size]
        imag = far[0, here, size:]
        power = real * real + imag * imag
        inverse = lax.rsqrt(jnp.maximum(power, 0.0625))
        factor = frame[here, :].astype(jnp.float32) * inverse - 1.0
        corr[here, :] = (factor * real).astype(jnp.bfloat16)
        low = pl.ds(pl.multiple_of(size + at, step), step)
        corr[low, :] = (factor * imag).astype(jnp.bfloat16)
        return carry

    lax.fori_loop(0, size // step, correct, 0)
    back[:, :size] = mdot(right[:size, :], corr[...]).astype(jnp.bfloat16)
    back[:, size:] = mdot(right[size:, :], corr[...]).astype(jnp.bfloat16)
    change[...] = mdot(back[...], left[...])

    row_at = offsets[slot, 0]
    fine = lax.rem(row_at, SUBLANES)
    coarse = row_at - fine
    tall = step + SUBLANES
    base = pl.multiple_of(slot * (cols // pl.num_programs(0)), LANES)
    shift = offsets[slot, 1] - base

    def spread(i, carry):
        at = pl.multiple_of(i * step, step)
        here = pl.ds(at, step)
        chg_real = change[here, :size]
        chg_imag = change[here, size:]
        ill_real = ill[0, here, :]
        ill_imag = ill[1, here, :]
        real = patch[0, 0, here, :]
        imag = patch[0, 1, here, :]
        numer[0, here, :] += real * chg_real + imag * chg_imag
        numer[1, here, :] += real * chg_imag - imag * chg_real
        grads = (
            ill_real * chg_real + ill_imag * chg_imag,
            ill_real * chg_imag - ill_imag * chg_real,
        )
        for part in range(2):
            moved = push_lanes(push_rows(grads[part], fine), shift)
            top = pl.multiple_of(coarse + at, SUBLANES)
            accum[part, pl.ds(top, tall), pl.ds(base, wide)] += moved
        return carry

    lax.fori_loop(0, size // step, spread, 0)

    @pl.when(slot == pl.num_programs(0) - 1)
    def _():
        upper[...] = accum[:, :rows, :cols]
        middle[...] = accum[:, rows : 2 * rows, :cols]
        lower[...] = accum[:, 2 * rows :, :cols]
        side[...] = accum[:, :, cols:]
        numer_out[...] = numer[...].astype(jnp.bfloat16)


def whole():
    return pl.BlockSpec(memory_space=pltpu.VMEM)


def forward(offsets, tiles, ill, left, right):
    slots = offsets.shape[0]
    size = ill.shape[-1]
    rows, cols = tiles[0].shape[1:]
    return pl.pallas_call(
        forward_kernel,
        grid=(slots,),
        in_specs=[pl.BlockSpec(memory_space=pltpu.SMEM)]
        + [pl.BlockSpec(memory_space=pl.ANY)] * 7
        + [whole()] * 3,
        out_specs=[
            pl.BlockSpec((1, size, 2 * size), lambda s: (s, 0, 0)),
            pl.BlockSpec((1, 2, size, size), lambda s: (s, 0, 0, 0)),
            pl.BlockSpec((2, size, size), lambda s: (0, 0, 0)),
        ],
        out_shape=[
            jax.ShapeDtypeStruct((slots, size, 2 * size), jnp.float32),
            jax.ShapeDtypeStruct((slots, 2, size, size), jnp.float32),
            jax.ShapeDtypeStruct((2, size, size), jnp.bfloat16),
        ],
        scratch_shapes=[
            pltpu.VMEM((2, 3 * rows, 2 * cols), jnp.float32),
            pltpu.VMEM((2 * size, size), jnp.bfloat16),
            pltpu.VMEM((size, 2 * size), jnp.bfloat16),
            pltpu.VMEM((size, size), jnp.float32),
            pltpu.SemaphoreType.DMA((6,)),
        ],
        compiler_params=pltpu.CompilerParams(vmem_limit_bytes=VMEM_LIMIT),
        cost_estimate=pl.CostEstimate(
            flops=16 * slots * size**3, bytes_accessed=28 * 2**20, transcendentals=0
        ),
        name="forward",
    )(offsets, *tiles, ill, left, right)


def backward(offsets, module_row, amp, far, patch, ill, left, right, rows, cols):
    slots = offsets.shape[0]
    size = ill.shape[-1]
    senders, _, own, depth, _ = amp.shape
    scalar = pl.BlockSpec(memory_space=pltpu.SMEM)
    tile = jax.ShapeDtypeStruct((2, rows, cols), jnp.float32)
    return pl.pallas_call(
        backward_kernel,
        grid=(slots,),
        in_specs=[
            scalar,
            scalar,
            pl.BlockSpec((senders, 1, own, depth, size), lambda s: (0, s, 0, 0, 0)),
            pl.BlockSpec((1, size, 2 * size), lambda s: (s, 0, 0)),
            pl.BlockSpec((1, 2, size, size), lambda s: (s, 0, 0, 0)),
            whole(),
            whole(),
            whole(),
        ],
        out_specs=[whole()] * 5,
        out_shape=[
            tile,
            tile,
            tile,
            jax.ShapeDtypeStruct((2, 3 * rows, cols), jnp.float32),
            jax.ShapeDtypeStruct((2, size, size), jnp.bfloat16),
        ],
        scratch_shapes=[
            pltpu.VMEM((size, size), jnp.bfloat16),
            pltpu.VMEM((2, 3 * rows, 2 * cols), jnp.float32),
            pltpu.VMEM((2 * size, size), jnp.bfloat16),
            pltpu.VMEM((size, 2 * size), jnp.bfloat16),
            pltpu.VMEM((size, 2 * size), jnp.float32),
            pltpu.VMEM((2, size, size), jnp.float32),
        ],
        compiler_params=pltpu.CompilerParams(vmem_limit_bytes=VMEM_LIMIT),
        cost_estimate=pl.CostEstimate(
            flops=16 * slots * size**3, bytes_accessed=28 * 2**20, transcendentals=0
        ),
        name="backward",
    )(offsets, module_row, amp, far, patch, ill, left, right)


def shard_sum(chunks):
    got = lax.all_to_all(chunks, ("row", "col"), split_axis=0, concat_axis=0, tiled=True)
    return jnp.sum(got.astype(jnp.float32), axis=0)


def shards(measured, module_row, scan_offsets, specimen, illumination):
    slots = scan_offsets.shape[2]
    size = illumination.shape[-1]
    rows, cols = specimen.shape[1:]
    n_row = lax.axis_size("row")
    devices = n_row * lax.axis_size("col")
    share_rows = 2 * size // devices
    offsets = scan_offsets.reshape(slots, 2)
    odd = lax.rem(lax.axis_index("row"), 2) == 1
    farther = passed_along(specimen, "row", -2)
    direct = lax.ppermute(specimen, "row", [(at + 1, at) for at in range(0, n_row, 2)])
    beside = passed_along(specimen, "col", -1)
    cut = measured.reshape((n_row, slots) + measured.shape[1:])
    cut, farther, direct, beside = lax.optimization_barrier((cut, farther, direct, beside))
    relayed = lax.ppermute(farther, "row", [(at, at + 1) for at in range(0, n_row, 2)])
    farther_beside = passed_along(farther, "col", -1)
    amp = lax.all_to_all(cut, "row", split_axis=0, concat_axis=0, tiled=True)
    below_beside = passed_along(jnp.where(odd, relayed, direct), "col", -1)
    cos_table, sin_table = dft_tables(size)
    left = jnp.asarray(np.block([[cos_table, -sin_table], [sin_table, cos_table]]))
    right = jnp.asarray(np.block([[cos_table, sin_table], [-sin_table, cos_table]]))
    tiles = (specimen, beside, direct, relayed, below_beside, farther, farther_beside)
    far, patch, density = forward(offsets, tiles, illumination, left, right)
    density_share = shard_sum(density.reshape(devices, share_rows, size))
    upper, middle, lower, side, numer = backward(
        offsets, module_row, amp, far, patch, illumination, left, right, rows, cols
    )
    numer_share = shard_sum(numer.reshape(devices, share_rows, size))
    got = passed_along(side, "col", 1)
    share = numer_share / jnp.sqrt(density_share + 1e-06)
    got, _ = lax.optimization_barrier((got, share))
    gathered = lax.all_gather(share, ("row", "col"), axis=0, tiled=True)
    middle = (middle + got[:, rows : 2 * rows]).astype(jnp.bfloat16)
    lower = (lower + got[:, 2 * rows :]).astype(jnp.bfloat16)
    middle = passed_along(middle, "row", 1).astype(jnp.float32)
    lower = passed_along(lower, "row", 2).astype(jnp.float32)
    specimen_step = upper + got[:, :rows] + middle + lower
    return (specimen_step, gathered.reshape(2, size, size))


def solution(mesh):
    return jax.shard_map(
        shards,
        mesh=mesh,
        in_specs=(
            P("col", "row", None, None),
            P(),
            P("row", "col", None, None),
            P(None, "row", "col"),
            P(),
        ),
        out_specs=(P(None, "row", "col"), P()),
        check_vma=False,
    )
```

```python
import math

import jax
import jax.numpy as jnp
import ml_dtypes
import numpy as np
from jax import lax
from jax.experimental import pallas as pl
from jax.experimental.pallas import tpu as pltpu
from jax.sharding import PartitionSpec as P

VMEM_LIMIT = 56 * 2**20
LANES = 128
SUBLANES = 8


def passed_along(value, axis, steps):
    count = lax.axis_size(axis)
    pairs = [(source, (source + steps) % count) for source in range(count)]
    return lax.ppermute(value, axis, pairs)


def dft_tables(size):
    index = np.arange(size, dtype=np.int32)
    wrapped = index[:, None] * index[None, :] % size
    angle = wrapped.astype(np.float32) * np.float32(2.0 * math.pi / size)
    norm = np.float32(1.0 / math.sqrt(size))
    return (
        (np.cos(angle) * norm).astype(ml_dtypes.bfloat16),
        (-np.sin(angle) * norm).astype(ml_dtypes.bfloat16),
    )


def pull_lanes(block, off):
    turn = lax.rem(LANES - off, LANES)
    lane = lax.broadcasted_iota(jnp.int32, (block.shape[0], LANES), 1)
    keep = lane < LANES - off
    count = block.shape[1] // LANES
    turned = [pltpu.roll(block[:, i * LANES : (i + 1) * LANES], turn, 1) for i in range(count)]
    return jnp.concatenate(
        [jnp.where(keep, turned[i], turned[i + 1]) for i in range(count - 1)], axis=1
    )


def push_lanes(block, off):
    lane = lax.broadcasted_iota(jnp.int32, (block.shape[0], LANES), 1)
    keep = lane >= off
    count = block.shape[1] // LANES
    blank = jnp.zeros((block.shape[0], LANES), block.dtype)
    turned = [pltpu.roll(block[:, i * LANES : (i + 1) * LANES], off, 1) for i in range(count)]
    turned = [blank] + turned + [blank]
    return jnp.concatenate(
        [jnp.where(keep, turned[i + 1], turned[i]) for i in range(count + 1)], axis=1
    )


def pull_rows(block, off):
    turn = lax.rem(SUBLANES - off, SUBLANES)
    row = lax.broadcasted_iota(jnp.int32, (SUBLANES, block.shape[1]), 0)
    keep = row < SUBLANES - off
    count = block.shape[0] // SUBLANES
    turned = [pltpu.roll(block[i * SUBLANES : (i + 1) * SUBLANES], turn, 0) for i in range(count)]
    return jnp.concatenate(
        [jnp.where(keep, turned[i], turned[i + 1]) for i in range(count - 1)], axis=0
    )


def push_rows(block, off):
    row = lax.broadcasted_iota(jnp.int32, (SUBLANES, block.shape[1]), 0)
    keep = row >= off
    count = block.shape[0] // SUBLANES
    blank = jnp.zeros((SUBLANES, block.shape[1]), block.dtype)
    turned = [pltpu.roll(block[i * SUBLANES : (i + 1) * SUBLANES], off, 0) for i in range(count)]
    turned = [blank] + turned + [blank]
    return jnp.concatenate(
        [jnp.where(keep, turned[i + 1], turned[i]) for i in range(count + 1)], axis=0
    )


def mdot(left, right):
    return jnp.dot(left, right, preferred_element_type=jnp.float32)


def forward_kernel(
    offsets, t00, t01, t10, t10_odd, t11, t20, t21, ill, left, right, far, patch, density_out,
    region, wave, half, density, sems,
):
    slot = pl.program_id(0)
    size = ill.shape[-1]
    rows, cols = t00.shape[1:]
    wide = size + LANES
    step = 64

    @pl.when(slot == 0)
    def _():
        def move(tile, at):
            down, across = divmod(at, 2)
            place = region.at[:, pl.ds(down * rows, rows), pl.ds(across * cols, cols)]
            return pltpu.make_async_copy(tile, place, sems.at[at])

        odd = lax.rem(lax.axis_index("row"), 2) == 1

        @pl.when(odd)
        def _():
            move(t10_odd, 2).start()

        @pl.when(jnp.logical_not(odd))
        def _():
            move(t10, 2).start()

        copies = [move(t00, 0), move(t01, 1), move(t11, 3), move(t20, 4), move(t21, 5)]
        for copy in copies:
            copy.start()
        for copy in copies:
            copy.wait()
        move(t10, 2).wait()
        density[...] = jnp.zeros_like(density)

    row_at = offsets[slot, 0]
    fine = lax.rem(row_at, SUBLANES)
    coarse = row_at - fine
    tall = step + SUBLANES
    base = pl.multiple_of(slot * (cols // pl.num_programs(0)), LANES)
    shift = offsets[slot, 1] - base

    def gather(i, carry):
        at = pl.multiple_of(i * step, step)
        here = pl.ds(at, step)
        parts = []
        for part in range(2):
            top = pl.multiple_of(coarse + at, SUBLANES)
            block = region[part, pl.ds(top, tall), pl.ds(base, wide)]
            parts.append(pull_rows(pull_lanes(block, shift), fine))
        real, imag = parts
        patch[0, 0, here, :] = real
        patch[0, 1, here, :] = imag
        density[here, :] += real * real + imag * imag
        ill_real = ill[0, here, :]
        ill_imag = ill[1, here, :]
        wave[here, :] = (ill_real * real - ill_imag * imag).astype(jnp.bfloat16)
        low = pl.ds(pl.multiple_of(size + at, step), step)
        wave[low, :] = (ill_real * imag + ill_imag * real).astype(jnp.bfloat16)
        return carry

    lax.fori_loop(0, size // step, gather, 0)
    half[:, :size] = mdot(left[:size, :], wave[...]).astype(jnp.bfloat16)
    half[:, size:] = mdot(left[size:, :], wave[...]).astype(jnp.bfloat16)
    far[0] = mdot(half[...], right[...])

    @pl.when(slot == pl.num_programs(0) - 1)
    def _():
        total = density[...].astype(jnp.bfloat16)
        density_out[0] = total
        density_out[1] = total


def backward_kernel(
    offsets, module_row, amp, far, patch, ill, left, right, upper, middle, lower, side, side_low, numer_out,
    frame, accum, corr, back, change, numer,
):
    slot = pl.program_id(0)
    size = ill.shape[-1]
    rows, cols = upper.shape[1:]
    wide = size + LANES
    step = 64
    senders, _, own, depth, _ = amp.shape

    @pl.when(slot == 0)
    def _():
        accum[...] = jnp.zeros_like(accum)
        numer[...] = jnp.zeros_like(numer)

    for sender in range(senders):
        for at in range(own):
            top = pl.multiple_of(module_row[sender * own + at] * depth, depth)
            frame[pl.ds(top, depth), :] = amp[sender, 0, at]

    def correct(i, carry):
        at = pl.multiple_of(i * step, step)
        here = pl.ds(at, step)
        real = far[0, here, :size]
        imag = far[0, here, size:]
        power = real * real + imag * imag
        inverse = lax.rsqrt(jnp.maximum(power, 0.0625))
        factor = frame[here, :].astype(jnp.float32) * inverse - 1.0
        corr[here, :] = (factor * real).astype(jnp.bfloat16)
        low = pl.ds(pl.multiple_of(size + at, step), step)
        corr[low, :] = (factor * imag).astype(jnp.bfloat16)
        return carry

    lax.fori_loop(0, size // step, correct, 0)
    back[:, :size] = mdot(right[:size, :], corr[...]).astype(jnp.bfloat16)
    back[:, size:] = mdot(right[size:, :], corr[...]).astype(jnp.bfloat16)
    change[...] = mdot(back[...], left[...])

    row_at = offsets[slot, 0]
    fine = lax.rem(row_at, SUBLANES)
    coarse = row_at - fine
    tall = step + SUBLANES
    base = pl.multiple_of(slot * (cols // pl.num_programs(0)), LANES)
    shift = offsets[slot, 1] - base

    def spread(i, carry):
        at = pl.multiple_of(i * step, step)
        here = pl.ds(at, step)
        chg_real = change[here, :size]
        chg_imag = change[here, size:]
        ill_real = ill[0, here, :]
        ill_imag = ill[1, here, :]
        real = patch[0, 0, here, :]
        imag = patch[0, 1, here, :]
        numer[0, here, :] += real * chg_real + imag * chg_imag
        numer[1, here, :] += real * chg_imag - imag * chg_real
        grads = (
            ill_real * chg_real + ill_imag * chg_imag,
            ill_real * chg_imag - ill_imag * chg_real,
        )
        for part in range(2):
            moved = push_lanes(push_rows(grads[part], fine), shift)
            top = pl.multiple_of(coarse + at, SUBLANES)
            accum[part, pl.ds(top, tall), pl.ds(base, wide)] += moved
        return carry

    lax.fori_loop(0, size // step, spread, 0)

    @pl.when(slot == pl.num_programs(0) - 1)
    def _():
        upper[...] = accum[:, :rows, :cols]
        middle[...] = accum[:, rows : 2 * rows, :cols]
        lower[...] = accum[:, 2 * rows :, :cols]
        side[...] = accum[:, :rows, cols:]
        side_low[...] = accum[:, rows:, cols:]
        numer_out[...] = numer[...].astype(jnp.bfloat16)


def whole():
    return pl.BlockSpec(memory_space=pltpu.VMEM)


def forward(offsets, tiles, ill, left, right):
    slots = offsets.shape[0]
    size = ill.shape[-1]
    rows, cols = tiles[0].shape[1:]
    return pl.pallas_call(
        forward_kernel,
        grid=(slots,),
        in_specs=[pl.BlockSpec(memory_space=pltpu.SMEM)]
        + [pl.BlockSpec(memory_space=pl.ANY)] * 7
        + [whole()] * 3,
        out_specs=[
            pl.BlockSpec((1, size, 2 * size), lambda s: (s, 0, 0)),
            pl.BlockSpec((1, 2, size, size), lambda s: (s, 0, 0, 0)),
            pl.BlockSpec((2, size, size), lambda s: (0, 0, 0)),
        ],
        out_shape=[
            jax.ShapeDtypeStruct((slots, size, 2 * size), jnp.float32),
            jax.ShapeDtypeStruct((slots, 2, size, size), jnp.float32),
            jax.ShapeDtypeStruct((2, size, size), jnp.bfloat16),
        ],
        scratch_shapes=[
            pltpu.VMEM((2, 3 * rows, 2 * cols), jnp.float32),
            pltpu.VMEM((2 * size, size), jnp.bfloat16),
            pltpu.VMEM((size, 2 * size), jnp.bfloat16),
            pltpu.VMEM((size, size), jnp.float32),
            pltpu.SemaphoreType.DMA((6,)),
        ],
        compiler_params=pltpu.CompilerParams(vmem_limit_bytes=VMEM_LIMIT),
        cost_estimate=pl.CostEstimate(
            flops=16 * slots * size**3, bytes_accessed=28 * 2**20, transcendentals=0
        ),
        name="forward",
    )(offsets, *tiles, ill, left, right)


def backward(offsets, module_row, amp, far, patch, ill, left, right, rows, cols):
    slots = offsets.shape[0]
    size = ill.shape[-1]
    senders, _, own, depth, _ = amp.shape
    scalar = pl.BlockSpec(memory_space=pltpu.SMEM)
    tile = jax.ShapeDtypeStruct((2, rows, cols), jnp.float32)
    return pl.pallas_call(
        backward_kernel,
        grid=(slots,),
        in_specs=[
            scalar,
            scalar,
            pl.BlockSpec((senders, 1, own, depth, size), lambda s: (0, s, 0, 0, 0)),
            pl.BlockSpec((1, size, 2 * size), lambda s: (s, 0, 0)),
            pl.BlockSpec((1, 2, size, size), lambda s: (s, 0, 0, 0)),
            whole(),
            whole(),
            whole(),
        ],
        out_specs=[whole()] * 6,
        out_shape=[
            tile,
            tile,
            tile,
            tile,
            jax.ShapeDtypeStruct((2, 2 * rows, cols), jnp.float32),
            jax.ShapeDtypeStruct((2, size, size), jnp.bfloat16),
        ],
        scratch_shapes=[
            pltpu.VMEM((size, size), jnp.bfloat16),
            pltpu.VMEM((2, 3 * rows, 2 * cols), jnp.float32),
            pltpu.VMEM((2 * size, size), jnp.bfloat16),
            pltpu.VMEM((size, 2 * size), jnp.bfloat16),
            pltpu.VMEM((size, 2 * size), jnp.float32),
            pltpu.VMEM((2, size, size), jnp.float32),
        ],
        compiler_params=pltpu.CompilerParams(vmem_limit_bytes=VMEM_LIMIT),
        cost_estimate=pl.CostEstimate(
            flops=16 * slots * size**3, bytes_accessed=28 * 2**20, transcendentals=0
        ),
        name="backward",
    )(offsets, module_row, amp, far, patch, ill, left, right)


def shard_sum(chunks):
    got = lax.all_to_all(chunks, ("row", "col"), split_axis=0, concat_axis=0, tiled=True)
    return jnp.sum(got.astype(jnp.float32), axis=0)


def shards(measured, module_row, scan_offsets, specimen, illumination):
    slots = scan_offsets.shape[2]
    size = illumination.shape[-1]
    rows, cols = specimen.shape[1:]
    n_row = lax.axis_size("row")
    devices = n_row * lax.axis_size("col")
    share_rows = 2 * size // devices
    offsets = scan_offsets.reshape(slots, 2)
    odd = lax.rem(lax.axis_index("row"), 2) == 1
    farther = passed_along(specimen, "row", -2)
    direct = lax.ppermute(specimen, "row", [(at + 1, at) for at in range(0, n_row, 2)])
    beside = passed_along(specimen, "col", -1)
    cut = measured.reshape((n_row, slots) + measured.shape[1:])
    farther, direct, beside = lax.optimization_barrier((farther, direct, beside))
    relayed = lax.ppermute(farther, "row", [(at, at + 1) for at in range(0, n_row, 2)])
    farther_beside = passed_along(farther, "col", -1)
    cut, relayed, farther_beside = lax.optimization_barrier((cut, relayed, farther_beside))
    amp = lax.all_to_all(cut, "row", split_axis=0, concat_axis=0, tiled=True)
    below_beside = passed_along(jnp.where(odd, relayed, direct), "col", -1)
    cos_table, sin_table = dft_tables(size)
    left = jnp.asarray(np.block([[cos_table, -sin_table], [sin_table, cos_table]]))
    right = jnp.asarray(np.block([[cos_table, sin_table], [-sin_table, cos_table]]))
    tiles = (specimen, beside, direct, relayed, below_beside, farther, farther_beside)
    far, patch, density = forward(offsets, tiles, illumination, left, right)
    density_share = shard_sum(density.reshape(devices, share_rows, size))
    upper, middle, lower, side, side_low, numer = backward(
        offsets, module_row, amp, far, patch, illumination, left, right, rows, cols
    )
    numer_share = shard_sum(numer.reshape(devices, share_rows, size))
    got_low = passed_along(side_low, "col", 1)
    share = numer_share / jnp.sqrt(density_share + 1e-06)
    got_low, side, _ = lax.optimization_barrier((got_low, side, share))
    gathered = lax.all_gather(share, ("row", "col"), axis=0, tiled=True)
    middle = (middle + got_low[:, :rows]).astype(jnp.bfloat16)
    lower = (lower + got_low[:, rows:]).astype(jnp.bfloat16)
    middle = passed_along(middle, "row", 1).astype(jnp.float32)
    lower = passed_along(lower, "row", 2).astype(jnp.float32)
    got = passed_along(side, "col", 1)
    specimen_step = upper + got + middle + lower
    return (specimen_step, gathered.reshape(2, size, size))


def solution(mesh):
    return jax.shard_map(
        shards,
        mesh=mesh,
        in_specs=(
            P("col", "row", None, None),
            P(),
            P("row", "col", None, None),
            P(None, "row", "col"),
            P(),
        ),
        out_specs=(P(None, "row", "col"), P()),
        check_vma=False,
    )
```
